256 devices in a mesh: dp: 64 (over z, x, core), mp: 4 (over y).
Axes of the slice: x: 4, y: 4, z: 8, core: 2. Of those that a mesh axis runs over, the one named last changes fastest.
Arguments:
- gradient: bfloat16 [64, 2, 256, 16384], P('dp', None, 'mp'), may hold values from -6 to 6
- momentum: float32 [64, 3, 256, 256], P('dp', None, 'mp'), may hold values from -6 to 6
- weights: float32 [2, 256, 16384], P(None, ('mp', 'dp')), may hold values from -6 to 6
- table: int32 [128, 1], replicated, may hold values from 0 to 63; in each aligned block of 128 rows (0 to 127, 128 to 255, ...) at most 3 rows name the same one
Outputs:
- new_momentum: float32 [64, 3, 256, 256], P('dp', None, 'mp')
- step_update: float32 [2, 256, 16384], P(None, ('mp', 'dp'))
- new_weights: float32 [2, 256, 16384], P(None, ('mp', 'dp'))
The draws below stay inside these ranges and needn't reach their ends.
Inputs may be any that keep to these rules, and one draw needn't show every extreme that they name: `table`: each owner is named by at most 3 head matrices, a bound that some block reaches; every owner by at least one.
All inputs are finite; a program needn't handle non-finite values.
Results may differ from the reference program's by a relative error of at most 0.0003.
Values may be sent and summed in bfloat16 or wider, within the bound.
No kernel may reach another device: no remote copies, remote signals or barrier semaphores. Data moves between devices by JAX's collectives and lax.ppermute only.
A program may use at most 64 MiB of HBM per device.

```python
import math
import jax
import jax.numpy as jnp
import numpy as np
from jax import lax

HEADS = 64
RANK = 256
L = 2
ITERS = 5
COLS = 256
MATS = 128
CAP = 3
N_DP = 64


def with_spikes(values, own_key, source, target, parts, factor):
    def block_of(position):
        return (jnp.arange(values.shape[position]) // (values.shape[position] // parts)).reshape((-1,) + (1,) * (values.ndim - 1 - position))

    one_side = jax.random.permutation(own_key, parts)[block_of(target)]
    far = (block_of(target) + parts // 2) % parts
    return jnp.where((block_of(source) == one_side) | (block_of(source) == far), factor * values, values)


def block_scale(stream_key, dims, split, smallest, high):
    gain, own = 1.0, jax.random.fold_in(stream_key, 6)
    for axis_at, shards_of in split:
        steps = jnp.exp(jax.random.uniform(jax.random.fold_in(own, axis_at), (shards_of,), jnp.float32, smallest / len(split), high / len(split)))
        gain = gain * jnp.repeat(steps, dims[axis_at] // shards_of).reshape([-1 if axis == axis_at else 1 for axis in range(len(dims))])
    return gain


def routed_block(stream_key, own, number, rows, count, top, reach, slope):
    sequence = jax.random.permutation(stream_key, count)
    packed, common = portions_of(count, rows * top, reach, slope, True), portions_of(count, rows * top, reach, slope, False)
    places = jnp.arange(count)

    def named(lengths, offset_by):
        used = int((lengths > 0).sum())
        fixed = max(1, used // 4)
        shifted = fixed + (places - fixed + offset_by * (used - fixed)) % max(1, count - fixed)
        return jnp.zeros((count,), jnp.int32).at[sequence[jnp.where(places < fixed, places, shifted)]].set(jnp.asarray(lengths, jnp.int32))

    lengths = jnp.where(number % 4 == 0, named(packed, number // 4), named(common, number - number // 4 - 1))
    mixed = jax.random.permutation(jax.random.fold_in(own, 3), count)
    giver, sink = mixed[0:count // 2 * 2:2], mixed[1:count // 2 * 2:2]
    slack = jnp.minimum(lengths[giver] - 1, reach - lengths[sink]) // 2
    slack = jnp.where((giver == sequence[0]) | (sink == sequence[0]) | (lengths[sink] == 0), 0, jnp.maximum(slack, 0))
    shifted = jax.random.randint(jax.random.fold_in(own, 4), (count // 2,), 0, 1 << 20) % (slack + 1)
    lengths = lengths.at[giver].add(-shifted).at[sink].add(shifted)
    members = jnp.searchsorted(jnp.cumsum(lengths), jnp.arange(rows * top), side="right").astype(jnp.int32)
    table = members.reshape(top, rows).T
    table = table[jax.random.permutation(jax.random.fold_in(own, 1), rows)]
    offset_by = jax.random.randint(jax.random.fold_in(own, 2), (rows, 1), 0, top)
    return jnp.take_along_axis(table, (jnp.arange(top)[None, :] + offset_by) % top, axis=1)


def portions_of(number_of, total, bound, lean, full):
    weights = [(1 << 20) // math.isqrt(grade ** lean) + 1 for grade in range(1, number_of + 1)]
    largest = bound if full else min(bound, max(-(-total // number_of), total * weights[0] // sum(weights)))
    least = 1 if total - largest >= number_of - 1 else 0
    given, rest = [largest] + [least] * (number_of - 1), total - largest - least * (number_of - 1)
    while rest > 0:
        movable = [i for i in range(1, number_of) if given[i] < largest] or [i for i in range(1, number_of) if given[i] < bound]
        pool, budget = sum([weights[i] for i in movable]), rest
        for i in movable:
            more = min(bound - given[i], max(1, budget * weights[i] // pool), rest)
            given[i] = given[i] + more
            rest = rest - more
    return np.array(given)


def scatter_about(rng, extent, deviation, limit, pieces=(), held_as=jnp.bfloat16):
    drawn = deviation * jax.random.normal(rng, extent, jnp.float32)
    if pieces:
        drawn = drawn * block_scale(rng, extent, pieces, -0.22, 0.18)
    return jnp.clip(drawn, -limit, limit).astype(held_as)


def noise_with(own_key, extent, spread, most, shards, heavy, held_as=jnp.bfloat16):
    drawn = spread * jax.random.normal(own_key, extent, jnp.float32)
    if shards:
        drawn = drawn * block_scale(own_key, extent, shards, -0.22, 0.18)
    return jnp.clip(with_spikes(drawn, jax.random.fold_in(own_key, 3), *heavy), -most, most).astype(held_as)


def setup_inputs(seed: int = 0) -> dict:
    key_of = jax.random.split(jax.random.key(seed), 5)
    gradient = noise_with(key_of[0], (N_DP, L, RANK, HEADS * COLS), 0.15, 6.0, ((0, 64), (2, 4)), (0, 2, 64, 4.0))
    momentum = scatter_about(key_of[1], (N_DP, CAP, RANK, COLS), 1.0, 6.0, ((0, 64), (2, 4)), jnp.float32)
    weights = scatter_about(key_of[2], (L, RANK, HEADS * COLS), 0.5, 6.0, ((1, 256),), jnp.float32)
    table_keys = jax.random.split(jax.random.fold_in(key_of[3], 1), MATS // MATS)
    table_turns = jax.random.permutation(jax.random.fold_in(key_of[3], 3), MATS // MATS)
    table = jax.vmap(lambda own, number: routed_block(jax.random.fold_in(key_of[3], 2), own, number, MATS, N_DP, 1, CAP, 2))(table_keys, table_turns).reshape((MATS, 1))
    return dict(gradient=gradient, momentum=momentum, weights=weights, table=table)


quintic_a = 3.4445
quintic_b = -4.775
quintic_c = 2.0315
momentum_beta = 0.95
learn_rate = 0.02
decay_rate = 0.1
rms_factor = 0.2
norm_epsilon = 1e-07

def placement(table, owner_count, capacity):
    owners = table[:, 0]
    count = owners.shape[0]
    index = jnp.arange(count, dtype=jnp.int32)
    before = (owners[:, None] == owners[None, :]) & (index[:, None] < index[None, :])
    slots = lax.optimization_barrier(jnp.sum(before.astype(jnp.int32), axis=0)).astype(jnp.int32)
    target = owners * capacity + slots
    rows = jnp.arange(owner_count * capacity, dtype=jnp.int32)
    return (rows[:, None] == target[None, :]).astype(jnp.float32)

def newton(advance):
    highest = lax.Precision.HIGHEST
    norm_value = jnp.sqrt(jnp.sum(advance * advance))
    iterate = advance / (norm_value + norm_epsilon)
    for turn_index in range(ITERS):
        gram_mat = jnp.dot(iterate.T, iterate, precision=highest)
        poly_mat = quintic_b * gram_mat + quintic_c * jnp.dot(gram_mat, gram_mat, precision=highest)
        iterate = quintic_a * iterate + jnp.dot(iterate, poly_mat, precision=highest)
    return iterate

def reference(gradient, momentum, weights, table):
    highest = lax.Precision.HIGHEST

    def accumulate(index, total):
        return total + lax.dynamic_index_in_dim(gradient, index, 0, keepdims=False).astype(jnp.float32)
    total = lax.fori_loop(0, N_DP, accumulate, jnp.zeros((L, RANK, HEADS * COLS), jnp.float32))
    matrices = total.reshape(L, RANK, HEADS, COLS).transpose(0, 2, 1, 3).reshape(MATS, RANK * COLS)
    chooser = placement(table, N_DP, CAP)
    live_mask = lax.optimization_barrier(jnp.sum(chooser, axis=1)) > 0
    slot_grads = jnp.dot(chooser, matrices, precision=highest).reshape(N_DP * CAP, RANK, COLS)
    previous = momentum.reshape(N_DP * CAP, RANK, COLS)
    fresh = jnp.where(live_mask[:, None, None], momentum_beta * previous + slot_grads, jnp.float32(0.0))
    advance = slot_grads + momentum_beta * fresh
    orthogonal = lax.map(newton, advance)
    direction = jnp.dot(chooser.T, orthogonal.reshape(N_DP * CAP, RANK * COLS), precision=highest)
    direction = direction.reshape(L, HEADS, RANK, COLS).transpose(0, 2, 1, 3).reshape(L, RANK, HEADS * COLS)
    scale = rms_factor * math.sqrt(max(RANK, COLS))
    step_update = scale * direction + decay_rate * weights
    new_weights = weights - learn_rate * step_update
    return (fresh.reshape(N_DP, CAP, RANK, COLS), step_update, new_weights)
```

```python
import math

import jax
import jax.numpy as jnp
from jax import lax
from jax.experimental import pallas as pl
from jax.experimental.pallas import tpu as pltpu
from jax.sharding import Mesh, PartitionSpec as P

HEADS = 64
RANK = 256
COLS = 256
L = 2
ITERS = 5
MATS = L * HEADS
CAP = 3
SPLIT = 46
REST = HEADS - SPLIT
NA = L * SPLIT
NB = L * REST
OWNERS = 64
DEVICES = 256
ALL = ("y", "z", "x", "core")

quintic_a = 3.4445
quintic_b = -4.775
quintic_c = 2.0315
momentum_beta = 0.95
learn_rate = 0.02
decay_rate = 0.1
rms_factor = 0.2
norm_epsilon = 1e-07
VMEM_LIMIT = 32 * 1024 * 1024

f32 = jnp.float32
bf16 = jnp.bfloat16


def targets(table):
    owners = table[:, 0]
    index = jnp.arange(MATS, dtype=jnp.int32)
    before = (owners[:, None] == owners[None, :]) & (index[:, None] < index[None, :])
    slots = jnp.sum(before.astype(jnp.int32), axis=0)
    return slots * OWNERS + owners


def vmem():
    return pl.BlockSpec(memory_space=pltpu.VMEM)


def smem():
    return pl.BlockSpec(memory_space=pltpu.SMEM)


def params():
    return pltpu.CompilerParams(vmem_limit_bytes=VMEM_LIMIT)


def spread_a_kernel(part_ref, out_ref):
    for half in range(2):
        for pair in range(4):
            for e in range(2):
                out_ref[half * 4 + pair, e * NA : (e + 1) * NA, :] = part_ref[
                    pl.ds(half * 8 + 2 * pair + e, NA, stride=16), :
                ]


def pack_kernel(target_ref, a_ref, b_ref, out_ref, sum_a, sum_b):
    sum_a[...] = jnp.sum(a_ref[...], axis=0)
    sum_b[...] = jnp.sum(b_ref[...], axis=0)
    out_ref[...] = jnp.zeros_like(out_ref)
    for layer in range(L):
        for head in range(HEADS):
            where = target_ref[layer * HEADS + head]
            for e in range(2):
                if head < SPLIT:
                    row = sum_a[pl.ds(e * NA + layer * SPLIT + head, 1), :]
                else:
                    row = sum_b[pl.ds(e * NB + layer * REST + head - SPLIT, 1), :]
                out_ref[pl.ds(where, 1), :, e * 128 : (e + 1) * 128] = row[None]


def update_kernel(flag_ref, got_ref, mom_ref, fresh_ref, adv_ref, grad):
    @pl.when(flag_ref[1] == 1)
    def _():
        for y in range(4):
            for half in range(2):
                for pair in range(4):
                    at = y * 64 + half * 32 + pair * 8
                    for e in range(2):
                        grad[half, pl.ds(y * 64 + 2 * pair + e, 8, stride=8), :] = got_ref[pl.ds(2 * at + e, 8, stride=2), :]

    @pl.when(flag_ref[1] == 0)
    def _():
        for y in range(4):
            for half in range(2):
                for e in range(2):
                    grad[half, pl.ds(y * 64 + e, 32, stride=2), :] = got_ref[pl.ds(2 * (y * 64 + half) + e, 32, stride=4), :]

    live = flag_ref[0] == 1
    for half in range(2):
        lanes = slice(half * 128, (half + 1) * 128)
        g = jnp.where(live, grad[half], 0.0)
        fresh = jnp.where(live, momentum_beta * mom_ref[:, lanes] + g, 0.0)
        fresh_ref[:, lanes] = fresh
        adv_ref[:, lanes] = g + momentum_beta * fresh


def halves(value):
    high = value.astype(bf16)
    return high, (value - high.astype(f32)).astype(bf16)


def times(left, right, transposed):
    dims = (((1,), (1 if transposed else 0,)), ((), ()))

    def dot(a, b):
        return lax.dot_general(a, b, dims, preferred_element_type=f32)

    (lh, ll), (rh, rl) = left, right
    return dot(lh, rh) + (dot(lh, rl) + dot(ll, rh))


def newton_kernel(adv_ref, out_ref):
    advance = adv_ref[...]
    norm = jnp.sqrt(jnp.sum(advance * advance))
    iterate = advance / (norm + norm_epsilon)
    for _ in range(ITERS):
        parts = halves(iterate)
        gram = times(parts, parts, True)
        gram_parts = halves(gram)
        poly = quintic_b * gram + quintic_c * times(gram_parts, gram_parts, False)
        iterate = quintic_a * iterate + times(halves(poly), parts, False)
    out_ref[...] = iterate


def finish_kernel(target_ref, got_ref, weights_ref, step_ref, new_ref):
    scale = rms_factor * math.sqrt(max(RANK, COLS))
    for layer in range(L):
        for head in range(HEADS):
            where = target_ref[layer * HEADS + head]
            lanes = slice(head * COLS, (head + 1) * COLS)
            held = weights_ref[layer, :, lanes]
            step = scale * got_ref[pl.ds(where, 1), 0, :] + decay_rate * held
            step_ref[layer, :, lanes] = step
            new_ref[layer, :, lanes] = held - learn_rate * step


def shape(*dims, dtype=f32):
    return jax.ShapeDtypeStruct(dims, dtype)


def on_device(gradient, momentum, weights, table):
    target = targets(table)
    me = lax.axis_index("y") * OWNERS + (lax.axis_index("z") * 4 + lax.axis_index("x")) * 2 + lax.axis_index("core")
    here = target == me
    live = jnp.any(here)
    first = jnp.any(here & (jnp.arange(MATS) % HEADS < SPLIT))
    flags = jnp.stack([live, first]).astype(jnp.int32)

    local = gradient[0].reshape(L, 8, 8, HEADS, 2, 128)
    part_a = local[:, :, :, :SPLIT].astype(f32).transpose(1, 0, 3, 4, 2, 5).reshape(8, NA * 16, 128)
    part_b = local[:, :, :, SPLIT:].transpose(1, 4, 0, 3, 2, 5).reshape(16, NB * 8, 128)
    sum_a = lax.psum_scatter(part_a, ("x", "core"), scatter_dimension=0, tiled=True)[0]
    got_b = lax.all_to_all(part_b, ("z", "core"), 0, 0, tiled=True)
    sum_b = jnp.sum(got_b.astype(f32), axis=0)
    send_b = sum_b.reshape(NB, 4, 2, 128).transpose(1, 2, 0, 3).reshape(4, 2 * NB, 128)
    last_b = lax.all_to_all(send_b, "x", 0, 0, tiled=True)
    held = jnp.concatenate([momentum[0], jnp.zeros((1, 64, COLS), f32)], axis=0)
    held = lax.all_to_all(held, "y", 0, 0, tiled=True).reshape(RANK, COLS)

    send_a = pl.pallas_call(
        spread_a_kernel, out_shape=shape(8, 2 * NA, 128), in_specs=[vmem()], out_specs=vmem(),
        compiler_params=params(), name="spread_a",
    )(sum_a)
    last_a = lax.all_to_all(send_a, "z", 0, 0, tiled=True)
    outgoing = pl.pallas_call(
        pack_kernel, out_shape=shape(DEVICES, 1, COLS), in_specs=[smem(), vmem(), vmem()], out_specs=vmem(),
        scratch_shapes=[pltpu.VMEM((2 * NA, 128), f32), pltpu.VMEM((2 * NB, 128), f32)],
        compiler_params=params(), name="pack",
    )(target, last_a, last_b)
    got = lax.all_to_all(outgoing, ALL, 0, 0, tiled=True).reshape(2 * DEVICES, 128)
    fresh, advance = pl.pallas_call(
        update_kernel, out_shape=(shape(RANK, COLS), shape(RANK, COLS)), in_specs=[smem(), vmem(), vmem()],
        out_specs=(vmem(), vmem()), scratch_shapes=[pltpu.VMEM((2, RANK, 128), f32)],
        compiler_params=params(), name="update",
    )(flags, got, held)
    new_momentum = lax.all_to_all(fresh.reshape(4, 64, COLS), "y", 0, 0, tiled=True)[:CAP]
    ortho = pl.pallas_call(
        newton_kernel, out_shape=shape(RANK, COLS), in_specs=[vmem()], out_specs=vmem(),
        compiler_params=params(), name="newton",
        cost_estimate=pl.CostEstimate(flops=15 * 3 * 2 * 256**3, bytes_accessed=2 << 18, transcendentals=0),
    )(advance)
    returned = lax.all_to_all(ortho.reshape(DEVICES, 1, COLS), ALL, 0, 0, tiled=True)
    step_update, new_weights = pl.pallas_call(
        finish_kernel, out_shape=(shape(L, 1, HEADS * COLS), shape(L, 1, HEADS * COLS)),
        in_specs=[smem(), vmem(), vmem()], out_specs=(vmem(), vmem()),
        compiler_params=params(), name="finish",
    )(target, returned, weights)
    return new_momentum[None], step_update, new_weights


def solution(mesh):
    fine = Mesh(mesh.devices.reshape(8, 4, 2, 4), ("z", "x", "core", "y"))
    dp = ("z", "x", "core")
    return jax.shard_map(
        on_device,
        mesh=fine,
        in_specs=(
            P(dp, None, "y", None),
            P(dp, None, "y", None),
            P(None, ("y",) + dp, None),
            P(),
        ),
        out_specs=(
            P(dp, None, "y", None),
            P(None, ("y",) + dp, None),
            P(None, ("y",) + dp, None),
        ),
        check_vma=False,
    )
```

```python
import math

import jax
import jax.numpy as jnp
from jax import lax
from jax.experimental import pallas as pl
from jax.experimental.pallas import tpu as pltpu
from jax.sharding import Mesh, PartitionSpec as P

HEADS = 64
RANK = 256
COLS = 256
L = 2
ITERS = 5
MATS = L * HEADS
CAP = 3
SPLIT = 48
REST = HEADS - SPLIT
NA = L * SPLIT
NB = L * REST
HALF = SPLIT // 2
NH = NA // 2
OWNERS = 64
DEVICES = 256
ALL = ("y", "z", "x", "core")

quintic_a = 3.4445
quintic_b = -4.775
quintic_c = 2.0315
momentum_beta = 0.95
learn_rate = 0.02
decay_rate = 0.1
rms_factor = 0.2
norm_epsilon = 1e-07
VMEM_LIMIT = 32 * 1024 * 1024

f32 = jnp.float32
bf16 = jnp.bfloat16


def targets(table):
    owners = table[:, 0]
    index = jnp.arange(MATS, dtype=jnp.int32)
    before = (owners[:, None] == owners[None, :]) & (index[:, None] < index[None, :])
    slots = jnp.sum(before.astype(jnp.int32), axis=0)
    return slots * OWNERS + owners


def vmem():
    return pl.BlockSpec(memory_space=pltpu.VMEM)


def smem():
    return pl.BlockSpec(memory_space=pltpu.SMEM)


def params():
    return pltpu.CompilerParams(vmem_limit_bytes=VMEM_LIMIT)


def lanes_of(head, half):
    return pl.ds(pl.multiple_of(head * COLS + half * 128, 128), 128)


def rows_of(block, size):
    return pl.ds(pl.multiple_of(block * size, size), size)


def x_bits():
    x = lax.axis_index("x")
    second = x // 2
    return (x + second) % 2, second


def split_kernel(grad_ref, cross_ref, b_ref):
    other = 1 - lax.axis_index("core")

    @pl.loop(0, REST // 2)
    def _(pair):
        head = SPLIT + 2 * pair
        for layer in range(L):
            for half in range(2):
                one = grad_ref[layer, :, lanes_of(head, half)].astype(f32)
                two = grad_ref[layer, :, lanes_of(head + 1, half)].astype(f32)
                at = rows_of(layer * (REST // 2) + pair, 16)
                for tile in range(8):
                    rows = slice(tile * 8, tile * 8 + 8)
                    b_ref[tile * 2 + half, at, :] = jnp.concatenate([one[rows], two[rows]], axis=0).astype(bf16)

    @pl.loop(0, SPLIT)
    def _(head):
        for layer in range(L):
            cross_ref[layer * SPLIT + head] = grad_ref[layer, :, lanes_of(head, other)]


def first_kernel(grad_ref, got_ref, send1_ref, keep1_ref, send2_ref, keep2_ref):
    core = lax.axis_index("core")
    one, two = x_bits()

    def total(layer, head, rows):
        mine = grad_ref[layer, rows, lanes_of(head, core)].astype(f32)
        return mine + got_ref[layer * SPLIT + head, rows, :].astype(f32)

    @pl.loop(0, HALF)
    def _(head):
        for layer in range(L):
            at = layer * HALF + head
            send1_ref[at] = total(layer, head, rows_of(1 - one, 32))
            keep1_ref[at] = total(layer, head, rows_of(one, 32))
            for block in range(2):
                rows = slice(block * 16, block * 16 + 16)
                send2_ref[at, rows, :] = total(layer, head + HALF, rows_of(2 * block + 1 - two, 16))
                keep2_ref[at, rows, :] = total(layer, head + HALF, rows_of(2 * block + two, 16))


def second_kernel(keep1_ref, got1_ref, keep2_ref, got2_ref, send1_ref, stay1_ref, send2_ref, stay2_ref):
    one, two = x_bits()

    @pl.loop(0, NH)
    def _(at):
        for rows, out in ((rows_of(1 - two, 16), send1_ref), (rows_of(two, 16), stay1_ref)):
            out[at] = keep1_ref[at, rows, :] + got1_ref[at, rows, :]
        for rows, out in ((rows_of(1 - one, 16), send2_ref), (rows_of(one, 16), stay2_ref)):
            out[at] = keep2_ref[at, rows, :] + got2_ref[at, rows, :]


def third_kernel(stay1_ref, got1_ref, stay2_ref, got2_ref, out_ref, total):
    total[: NH * 16, :] = (stay1_ref[...] + got1_ref[...]).reshape(NH * 16, 128)
    total[NH * 16 :, :] = (stay2_ref[...] + got2_ref[...]).reshape(NH * 16, 128)
    for pair in range(8):
        for e in range(2):
            out_ref[pair, e * NA : (e + 1) * NA, :] = total[pl.ds(2 * pair + e, NA, stride=16), :]


def b_kernel(part_ref, mom_ref, own_ref, near_ref, far_ref, across_ref, mom1_ref, mom2_ref, mom3_ref, total):
    total[...] = part_ref[0].astype(f32)
    for source in range(1, 16):
        total[...] += part_ref[source].astype(f32)
    x, y = lax.axis_index("x"), lax.axis_index("y")
    for pair, out in ((x, own_ref), (x + 1 - 2 * (x % 2), near_ref), (3 - x, far_ref), ((x + 2) % 4, across_ref)):
        for e in range(2):
            out[e * NB : (e + 1) * NB, :] = total[pl.ds(2 * pair + e, NB, stride=8), :]
    for step, out in ((1, mom1_ref), (2, mom2_ref), (3, mom3_ref)):
        out[...] = mom_ref[jnp.minimum((y + step) % 4, CAP - 1)]


def pack_kernel(target_ref, a_ref, own_ref, near_ref, far_ref, across_ref, out_ref, sum_a, sum_b):
    sum_a[...] = jnp.sum(a_ref[...], axis=0)
    sum_b[...] = (own_ref[...] + near_ref[...]) + (far_ref[...] + across_ref[...])
    out_ref[...] = jnp.zeros_like(out_ref)
    for layer in range(L):
        for head in range(HEADS):
            where = target_ref[layer * HEADS + head]
            for e in range(2):
                if head < HALF:
                    row = sum_a[pl.ds(e * NA + layer * HALF + head, 1), :]
                elif head < SPLIT:
                    row = sum_a[pl.ds(e * NA + NH + layer * HALF + head - HALF, 1), :]
                else:
                    row = sum_b[pl.ds(e * NB + layer * REST + head - SPLIT, 1), :]
                out_ref[pl.ds(where, 1), :, e * 128 : (e + 1) * 128] = row[None]


def halves(value):
    high = value.astype(bf16)
    return high, (value - high.astype(f32)).astype(bf16)


def times(left, right, transposed):
    dims = (((1,), (1 if transposed else 0,)), ((), ()))

    def dot(a, b):
        return lax.dot_general(a, b, dims, preferred_element_type=f32)

    (lh, ll), (rh, rl) = left, right
    return dot(lh, rh) + (dot(lh, rl) + dot(ll, rh))


def newton(advance):
    norm = jnp.sqrt(jnp.sum(advance * advance))
    iterate = advance / (norm + norm_epsilon)
    for _ in range(ITERS):
        parts = halves(iterate)
        gram = times(parts, parts, True)
        gram_parts = halves(gram)
        poly = quintic_b * gram + quintic_c * times(gram_parts, gram_parts, False)
        iterate = quintic_a * iterate + times(halves(poly), parts, False)
    return iterate


def work_kernel(target_ref, got_ref, held_ref, mom1_ref, mom2_ref, mom3_ref, out_ref, own_ref, new1_ref, new2_ref, new3_ref, grad, fresh, adv):
    y = lax.axis_index("y")
    me = y * OWNERS + (lax.axis_index("z") * 4 + lax.axis_index("x")) * 2 + lax.axis_index("core")
    index = lax.broadcasted_iota(jnp.int32, (1, MATS), 1)
    kind = jnp.where(target_ref[...] == me, jnp.where(index % HEADS < SPLIT, 2, 1), 0)
    kind = jnp.max(kind)

    @pl.when(kind == 2)
    def _():
        for block in range(4):
            for x, (one, two) in enumerate(((0, 0), (1, 0), (1, 1), (0, 1))):
                for half in range(2):
                    for e in range(2):
                        grad[half, pl.ds(block * 64 + one * 32 + two * 16 + e, 8, stride=2), :] = got_ref[
                            pl.ds(2 * (block * 64 + x * 2 + half) + e, 8, stride=16), :
                        ]

    @pl.when(kind != 2)
    def _():
        for block in range(4):
            for half in range(2):
                for e in range(2):
                    grad[half, pl.ds(block * 64 + e, 32, stride=2), :] = got_ref[pl.ds(2 * (block * 64 + half) + e, 32, stride=4), :]

    live = kind > 0
    for step, mom_ref in enumerate((None, mom1_ref, mom2_ref, mom3_ref)):
        rows = rows_of((y + 4 - step) % 4, 64)
        mom = held_ref[jnp.minimum(y, CAP - 1)] if mom_ref is None else mom_ref[...]
        for half in range(2):
            lanes = slice(half * 128, (half + 1) * 128)
            g = jnp.where(live, grad[half, rows, :], 0.0)
            new = jnp.where(live, momentum_beta * mom[:, lanes] + g, 0.0)
            fresh[rows, lanes] = new
            adv[rows, lanes] = g + momentum_beta * new
    for step, out in enumerate((own_ref, new1_ref, new2_ref, new3_ref)):
        out[...] = fresh[rows_of((y + step) % 4, 64), :]
    ortho = newton(adv[...])
    for half in range(2):
        out_ref[pl.ds(half, RANK, stride=2), :] = ortho[:, half * 128 : (half + 1) * 128]


def finish_kernel(target_ref, got_ref, weights_ref, own_ref, new1_ref, new2_ref, new3_ref, mom_ref, step_ref, new_ref):
    y = lax.axis_index("y")
    for step, ref in enumerate((own_ref, new1_ref, new2_ref, new3_ref)):
        slot = (y + 4 - step) % 4

        @pl.when(slot < CAP)
        def _(slot=slot, ref=ref):
            mom_ref[slot] = ref[...]

    scale = rms_factor * math.sqrt(max(RANK, COLS))
    for layer in range(L):
        for head in range(HEADS):
            where = target_ref[layer * HEADS + head]
            lanes = slice(head * COLS, (head + 1) * COLS)
            held = weights_ref[layer, :, lanes]
            step = scale * got_ref[pl.ds(where, 1), 0, :] + decay_rate * held
            step_ref[layer, :, lanes] = step
            new_ref[layer, :, lanes] = held - learn_rate * step


def shape(*dims, dtype=f32):
    return jax.ShapeDtypeStruct(dims, dtype)


def call(kernel, outs, ins, scratch=(), flops=0, moved=1 << 22):
    many = isinstance(outs, tuple)
    return pl.pallas_call(
        kernel,
        out_shape=outs,
        in_specs=[smem() if kind == "s" else vmem() for kind in ins],
        out_specs=tuple(vmem() for _ in outs) if many else vmem(),
        scratch_shapes=[pltpu.VMEM(dims, f32) for dims in scratch],
        compiler_params=params(),
        cost_estimate=pl.CostEstimate(flops=flops, bytes_accessed=moved, transcendentals=0),
        name=kernel.__name__.removesuffix("_kernel"),
    )


NEAR = [(i, i ^ 1) for i in range(4)]
FAR = [(i, 3 - i) for i in range(4)]
ACROSS = [(i, (i + 2) % 4) for i in range(4)]


def along_y(values):
    return [
        lax.ppermute(value, "y", [(i, (i + step) % 4) for i in range(4)]) for step, value in enumerate(values, start=1)
    ]


def on_device(gradient, momentum, weights, table):
    target = targets(table)
    local = gradient[0]

    cross, part_b = call(split_kernel, (shape(NA, 64, 128, dtype=bf16), shape(16, NB * 8, 128, dtype=bf16)), "v")(local)
    crossed = lax.ppermute(cross, "core", [(0, 1), (1, 0)])
    got_b = lax.all_to_all(part_b, ("z", "core"), 0, 0, tiled=True)
    send1, keep1, send2, keep2 = call(first_kernel, (shape(NH, 32, 128),) * 4, "vv")(local, crossed)
    got1, got2 = lax.ppermute(send1, "x", NEAR), lax.ppermute(send2, "x", FAR)
    send1, stay1, send2, stay2 = call(second_kernel, (shape(NH, 16, 128),) * 4, "vvvv")(keep1, got1, keep2, got2)
    got1, got2 = lax.ppermute(send1, "x", FAR), lax.ppermute(send2, "x", NEAR)
    send_a = call(third_kernel, shape(8, 2 * NA, 128), "vvvv", [(NA * 16, 128)])(stay1, got1, stay2, got2)
    last_a = lax.all_to_all(send_a, "z", 0, 0, tiled=True)

    outs = (shape(2 * NB, 128),) * 4 + (shape(64, COLS),) * 3
    own, near, far, across, *moms = call(b_kernel, outs, "vv", [(NB * 8, 128)])(got_b, momentum[0])
    near, far, across = lax.ppermute(near, "x", NEAR), lax.ppermute(far, "x", FAR), lax.ppermute(across, "x", ACROSS)
    moms = along_y(moms)

    outgoing = call(pack_kernel, shape(DEVICES, 1, COLS), "svvvvv", [(2 * NA, 128), (2 * NB, 128)])(
        target, last_a, own, near, far, across
    )
    got = lax.all_to_all(outgoing, ALL, 0, 0, tiled=True).reshape(2 * DEVICES, 128)
    outs = (shape(2 * RANK, 128),) + (shape(64, COLS),) * 4
    scratch = [(2, RANK, 128), (RANK, COLS), (RANK, COLS)]
    ortho, fresh, *news = call(work_kernel, outs, "vvvvvv", scratch, 15 * 3 * 2 * 256**3)(
        target.reshape(1, MATS), got, momentum[0], *moms
    )
    returned = lax.all_to_all(ortho.reshape(DEVICES, 1, COLS), ALL, 0, 0, tiled=True)
    news = along_y(news)
    outs = (shape(CAP, 64, COLS), shape(L, 1, HEADS * COLS), shape(L, 1, HEADS * COLS))
    new_momentum, step_update, new_weights = call(finish_kernel, outs, "svvvvvv")(target, returned, weights, fresh, *news)
    return new_momentum[None], step_update, new_weights


def solution(mesh):
    fine = Mesh(mesh.devices.reshape(8, 4, 2, 4), ("z", "x", "core", "y"))
    dp = ("z", "x", "core")
    return jax.shard_map(
        on_device,
        mesh=fine,
        in_specs=(
            P(dp, None, "y", None),
            P(dp, None, "y", None),
            P(None, ("y",) + dp, None),
            P(),
        ),
        out_specs=(
            P(dp, None, "y", None),
            P(None, ("y",) + dp, None),
            P(None, ("y",) + dp, None),
        ),
        check_vma=False,
    )
```

```python
import math

import jax
import jax.numpy as jnp
from jax import lax
from jax.experimental import pallas as pl
from jax.experimental.pallas import tpu as pltpu
from jax.sharding import Mesh, PartitionSpec as P

HEADS = 64
RANK = 256
COLS = 256
L = 2
ITERS = 5
MATS = L * HEADS
CAP = 3
GROUP = HEADS // 4
NG = L * GROUP
OWNERS = 64
DEVICES = 256
ALL = ("y", "z", "x", "core")

quintic_a = 3.4445
quintic_b = -4.775
quintic_c = 2.0315
momentum_beta = 0.95
learn_rate = 0.02
decay_rate = 0.1
rms_factor = 0.2
norm_epsilon = 1e-07
VMEM_LIMIT = 32 * 1024 * 1024

f32 = jnp.float32
bf16 = jnp.bfloat16


def targets(table):
    owners = table[:, 0]
    index = jnp.arange(MATS, dtype=jnp.int32)
    before = (owners[:, None] == owners[None, :]) & (index[:, None] < index[None, :])
    slots = jnp.sum(before.astype(jnp.int32), axis=0)
    return slots * OWNERS + owners


def params():
    return pltpu.CompilerParams(vmem_limit_bytes=VMEM_LIMIT)


def lanes_of(head, half):
    return pl.ds(pl.multiple_of(head * COLS + half * 128, 128), 128)


def rows_of(block, size):
    return pl.ds(pl.multiple_of(block * size, size), size)


def bits():
    x = lax.axis_index("x")
    second = x // 2
    return (x + second) % 2, second, lax.axis_index("z") % 2


def cross_kernel(grad_ref, cross_ref):
    other = 1 - lax.axis_index("core")

    @pl.loop(0, HEADS)
    def _(head):
        for layer in range(L):
            cross_ref[layer * HEADS + head] = grad_ref[layer, :, lanes_of(head, other)]


def first_kernel(grad_ref, got_ref, mom_ref, *refs):
    send1, keep1, send2, keep2, send3, keep3, send4, keep4, mom1, mom2, mom3 = refs
    core = lax.axis_index("core")
    one, two, three = bits()

    def total(layer, head, rows):
        mine = grad_ref[layer, rows, lanes_of(head, core)].astype(f32)
        return mine + got_ref[layer * HEADS + head, rows, :].astype(f32)

    @pl.loop(0, GROUP)
    def _(head):
        for layer in range(L):
            at = layer * GROUP + head
            send1[at] = total(layer, head, rows_of(1 - one, 32))
            keep1[at] = total(layer, head, rows_of(one, 32))
            for block in range(2):
                rows = slice(block * 16, block * 16 + 16)
                send2[at, rows, :] = total(layer, GROUP + head, rows_of(2 * block + 1 - two, 16))
                keep2[at, rows, :] = total(layer, GROUP + head, rows_of(2 * block + two, 16))
            for group, send, keep in ((2, send3, keep3), (3, send4, keep4)):
                for block in range(4):
                    rows = slice(block * 8, block * 8 + 8)
                    both = total(layer, group * GROUP + head, slice(block * 16, block * 16 + 16))
                    send[at, rows, :] = jnp.where(three == 0, both[8:], both[:8])
                    keep[at, rows, :] = jnp.where(three == 0, both[:8], both[8:])

    y = lax.axis_index("y")
    for step, out in ((1, mom1), (2, mom2), (3, mom3)):
        out[...] = mom_ref[jnp.minimum((y + step) % 4, CAP - 1)]


def second_kernel(*refs):
    one, two, three = bits()
    keeps, gots, sends, stays = refs[0:4], refs[4:8], refs[8:12], refs[12:16]

    @pl.loop(0, NG)
    def _(at):
        for group, bit in ((0, three), (1, three), (3, two)):
            for block in range(2):
                rows = slice(block * 8, block * 8 + 8)
                for value, outs in ((1 - bit, sends), (bit, stays)):
                    here = rows_of(2 * block + value, 8)
                    outs[group][at, rows, :] = keeps[group][at, here, :] + gots[group][at, here, :]
        for value, outs in ((1 - one, sends), (one, stays)):
            here = rows_of(value, 16)
            outs[2][at] = keeps[2][at, here, :] + gots[2][at, here, :]


def third_kernel(*refs):
    one, two, _ = bits()
    stays, gots, (send_far, keep_far, send_near, keep_near) = refs[0:4], refs[4:8], refs[8:12]

    @pl.loop(0, NG)
    def _(at):
        for group, bit, send, keep in ((0, two, send_far, keep_far), (2, two, send_far, keep_far), (1, one, send_near, keep_near), (3, one, send_near, keep_near)):
            to = (group // 2) * NG + at
            for value, out in ((1 - bit, send), (bit, keep)):
                here = rows_of(value, 8)
                out[to] = stays[group][at, here, :] + gots[group][at, here, :]


def pack_kernel(target_ref, far_ref, got_far_ref, near_ref, got_near_ref, out_ref):
    out_ref[...] = jnp.zeros_like(out_ref)
    for layer in range(L):
        for head in range(HEADS):
            where = target_ref[layer * HEADS + head]
            group = head // GROUP
            at = (group // 2) * NG + layer * GROUP + head % GROUP
            kept, got = (far_ref, got_far_ref) if group % 2 == 0 else (near_ref, got_near_ref)
            out_ref[where] = kept[at] + got[at]


def halves(value):
    high = value.astype(bf16)
    return high, (value - high.astype(f32)).astype(bf16)


def times(left, right, transposed):
    dims = (((1,), (1 if transposed else 0,)), ((), ()))

    def dot(a, b):
        return lax.dot_general(a, b, dims, preferred_element_type=f32)

    (lh, ll), (rh, rl) = left, right
    return dot(lh, rh) + (dot(lh, rl) + dot(ll, rh))


def newton(advance):
    norm = jnp.sqrt(jnp.sum(advance * advance))
    iterate = advance / (norm + norm_epsilon)
    for _ in range(ITERS):
        parts = halves(iterate)
        gram = times(parts, parts, True)
        gram_parts = halves(gram)
        poly = quintic_b * gram + quintic_c * times(gram_parts, gram_parts, False)
        iterate = quintic_a * iterate + times(halves(poly), parts, False)
    return iterate


def work_kernel(target_ref, got_ref, held_ref, mom1_ref, mom2_ref, mom3_ref, out_ref, own_ref, new1_ref, new2_ref, new3_ref, fresh, adv):
    y = lax.axis_index("y")
    me = y * OWNERS + (lax.axis_index("z") * 4 + lax.axis_index("x")) * 2 + lax.axis_index("core")
    live = jnp.max(jnp.where(target_ref[...] == me, 1, 0)) > 0
    for step, mom_ref in enumerate((None, mom1_ref, mom2_ref, mom3_ref)):
        block = (y + 4 - step) % 4
        for x, (one, two) in enumerate(((0, 0), (1, 0), (1, 1), (0, 1))):
            for three in range(2):
                tile = 4 * one + 2 * two + three
                for half in range(2):
                    lanes = slice(half * 128, (half + 1) * 128)
                    parts = [got_ref[block * 64 + (z * 4 + x) * 2 + half] for z in range(three, 8, 2)]
                    g = jnp.where(live, (parts[0] + parts[1]) + (parts[2] + parts[3]), 0.0)
                    if mom_ref is None:
                        mom = held_ref[jnp.minimum(y, CAP - 1), tile * 8 : tile * 8 + 8, lanes]
                    else:
                        mom = mom_ref[tile * 8 : tile * 8 + 8, lanes]
                    new = jnp.where(live, momentum_beta * mom + g, 0.0)
                    rows = rows_of(block * 8 + tile, 8)
                    fresh[rows, lanes] = new
                    adv[rows, lanes] = g + momentum_beta * new
    for step, out in enumerate((own_ref, new1_ref, new2_ref, new3_ref)):
        out[...] = fresh[rows_of((y + step) % 4, 64), :]
    ortho = newton(adv[...])
    for half in range(2):
        out_ref[pl.ds(half, RANK, stride=2), :] = ortho[:, half * 128 : (half + 1) * 128]


def finish_kernel(target_ref, got_ref, weights_ref, own_ref, new1_ref, new2_ref, new3_ref, mom_ref, step_ref, new_ref):
    y = lax.axis_index("y")
    for step, ref in enumerate((own_ref, new1_ref, new2_ref, new3_ref)):
        slot = (y + 4 - step) % 4

        @pl.when(slot < CAP)
        def _(slot=slot, ref=ref):
            mom_ref[slot] = ref[...]

    scale = rms_factor * math.sqrt(max(RANK, COLS))
    for layer in range(L):
        for head in range(HEADS):
            where = target_ref[layer * HEADS + head]
            lanes = slice(head * COLS, (head + 1) * COLS)
            held = weights_ref[layer, :, lanes]
            step = scale * got_ref[pl.ds(where, 1), 0, :] + decay_rate * held
            step_ref[layer, :, lanes] = step
            new_ref[layer, :, lanes] = held - learn_rate * step


def shape(*dims, dtype=f32):
    return jax.ShapeDtypeStruct(dims, dtype)


def call(kernel, outs, ins, scratch=(), flops=0, moved=1 << 22):
    many = isinstance(outs, tuple)
    out_spec = pl.BlockSpec(memory_space=pltpu.VMEM)
    return pl.pallas_call(
        kernel,
        out_shape=outs,
        in_specs=[pl.BlockSpec(memory_space=pltpu.SMEM if kind == "s" else pltpu.VMEM) for kind in ins],
        out_specs=tuple(out_spec for _ in outs) if many else out_spec,
        scratch_shapes=[pltpu.VMEM(dims, f32) for dims in scratch],
        compiler_params=params(),
        cost_estimate=pl.CostEstimate(flops=flops, bytes_accessed=moved, transcendentals=0),
        name=kernel.__name__.removesuffix("_kernel"),
    )


NEAR = [(i, i ^ 1) for i in range(4)]
FAR = [(i, 3 - i) for i in range(4)]
PAIR = [(i, i ^ 1) for i in range(8)]
LINK = [(i, (i + 1 if i % 2 else i - 1) % 8) for i in range(8)]


def along_y(values):
    return [
        lax.ppermute(value, "y", [(i, (i + step) % 4) for i in range(4)]) for step, value in enumerate(values, start=1)
    ]


def on_device(gradient, momentum, weights, table):
    target = targets(table)
    local = gradient[0]

    cross = call(cross_kernel, shape(MATS, 64, 128, dtype=bf16), "v")(local)
    crossed = lax.ppermute(cross, "core", [(0, 1), (1, 0)])
    outs = (shape(NG, 32, 128),) * 8 + (shape(64, COLS),) * 3
    *parts, mom1, mom2, mom3 = call(first_kernel, outs, "vvv")(local, crossed, momentum[0])
    sends, keeps = parts[0::2], parts[1::2]
    moves = (("x", NEAR), ("x", FAR), ("z", PAIR), ("z", LINK))
    gots = [lax.ppermute(value, *move) for value, move in zip(sends, moves)]
    moms = along_y((mom1, mom2, mom3))

    parts = call(second_kernel, (shape(NG, 16, 128),) * 8, "v" * 8)(*keeps, *gots)
    sends, stays = parts[:4], parts[4:]
    moves = (("z", PAIR), ("z", LINK), ("x", NEAR), ("x", FAR))
    gots = [lax.ppermute(value, *move) for value, move in zip(sends, moves)]

    send_far, keep_far, send_near, keep_near = call(third_kernel, (shape(2 * NG, 8, 128),) * 4, "v" * 8)(*stays, *gots)
    got_far, got_near = lax.ppermute(send_far, "x", FAR), lax.ppermute(send_near, "x", NEAR)

    outgoing = call(pack_kernel, shape(DEVICES, 8, 128), "svvvv")(target, keep_far, got_far, keep_near, got_near)
    got = lax.all_to_all(outgoing, ALL, 0, 0, tiled=True)
    outs = (shape(2 * RANK, 128),) + (shape(64, COLS),) * 4
    ortho, fresh, *news = call(work_kernel, outs, "vvvvvv", [(RANK, COLS), (RANK, COLS)], 15 * 3 * 2 * 256**3)(
        target.reshape(1, MATS), got, momentum[0], *moms
    )
    returned = lax.all_to_all(ortho.reshape(DEVICES, 1, COLS), ALL, 0, 0, tiled=True)
    news = along_y(news)
    outs = (shape(CAP, 64, COLS), shape(L, 1, HEADS * COLS), shape(L, 1, HEADS * COLS))
    new_momentum, step_update, new_weights = call(finish_kernel, outs, "svvvvvv")(target, returned, weights, fresh, *news)
    return new_momentum[None], step_update, new_weights


def solution(mesh):
    fine = Mesh(mesh.devices.reshape(8, 4, 2, 4), ("z", "x", "core", "y"))
    dp = ("z", "x", "core")
    return jax.shard_map(
        on_device,
        mesh=fine,
        in_specs=(
            P(dp, None, "y", None),
            P(dp, None, "y", None),
            P(None, ("y",) + dp, None),
            P(),
        ),
        out_specs=(
            P(dp, None, "y", None),
            P(None, ("y",) + dp, None),
            P(None, ("y",) + dp, None),
        ),
        check_vma=False,
    )
```

```python
import functools
import math

import jax
import jax.numpy as jnp
from jax import lax
from jax.experimental import pallas as pl
from jax.experimental.pallas import tpu as pltpu
from jax.sharding import Mesh, PartitionSpec as P

HEADS = 64
RANK = 256
COLS = 256
L = 2
ITERS = 5
MATS = L * HEADS
CAP = 3
SIZE = HEADS // 2
COUNT = L * SIZE
OWNERS = 64
DEVICES = 256
ALL = ("y", "z", "x", "core")

quintic_a = 3.4445
quintic_b = -4.775
quintic_c = 2.0315
momentum_beta = 0.95
learn_rate = 0.02
decay_rate = 0.1
rms_factor = 0.2
norm_epsilon = 1e-07
VMEM_LIMIT = 32 * 1024 * 1024

f32 = jnp.float32
bf16 = jnp.bfloat16


def targets(table):
    owners = table[:, 0]
    index = jnp.arange(MATS, dtype=jnp.int32)
    before = (owners[:, None] == owners[None, :]) & (index[:, None] < index[None, :])
    slots = jnp.sum(before.astype(jnp.int32), axis=0)
    return slots * OWNERS + owners


def params():
    return pltpu.CompilerParams(vmem_limit_bytes=VMEM_LIMIT)


def lanes_of(head, half):
    return pl.ds(pl.multiple_of(head * COLS + half * 128, 128), 128)


def rows_of(block, size):
    return pl.ds(pl.multiple_of(block * size, size), size)


def bits():
    x = lax.axis_index("x")
    second = x // 2
    return (x + second) % 2, second, lax.axis_index("z") % 2


def middle_bit(group):
    one, two, three = bits()
    return jnp.where(lax.axis_index("core") == 0, three, two if group else one)


def rows_kernel(first, size, mine, grad_ref, out_ref, sems):
    core = lax.axis_index("core")
    rows = rows_of(core if mine else 1 - core, 32)
    lanes = slice(first * COLS, (first + size) * COLS)
    copies = [pltpu.make_async_copy(grad_ref.at[layer, rows, lanes], out_ref.at[layer], sems.at[layer]) for layer in range(L)]
    for copy in copies:
        copy.start()
    for copy in copies:
        copy.wait()


def total(own_ref, got_ref, layer, rows, lanes):
    return own_ref[layer, rows, lanes].astype(f32) + got_ref[layer, rows, lanes].astype(f32)


def first_kernel(group, own_ref, got_ref, send, keep):
    one, two, three = bits()

    @pl.when(lax.axis_index("core") == 0)
    def _():
        @pl.loop(0, SIZE, unroll=2)
        def _(head):
            for layer in range(L):
                at = layer * SIZE + head
                for value, out in ((1 - (two if group else one), send), ((two if group else one), keep)):
                    for block in range(2):
                        if group:
                            both = total(own_ref, got_ref, layer, slice(block * 16, block * 16 + 16), lanes_of(head, value))
                        else:
                            both = total(own_ref, got_ref, layer, rows_of(value, 16), lanes_of(head, block))
                        out[at, 2 * block] = both[:8]
                        out[at, 2 * block + 1] = both[8:]

    @pl.when(lax.axis_index("core") == 1)
    def _():
        @pl.loop(0, SIZE, unroll=2)
        def _(head):
            for layer in range(L):
                at = layer * SIZE + head
                for row in range(2):
                    for lane in range(2):
                        both = total(own_ref, got_ref, layer, slice(row * 16, row * 16 + 16), lanes_of(head, lane))
                        tile = 2 * row + lane if group else 2 * lane + row
                        send[at, tile] = jnp.where(three == 0, both[8:], both[:8])
                        keep[at, tile] = jnp.where(three == 0, both[:8], both[8:])


def second_kernel(group, kept, got, send, keep):
    bit = middle_bit(group)

    @pl.loop(0, COUNT, unroll=4)
    def _(at):
        for block in range(2):
            for tile, out in ((2 * block + 1 - bit, send), (2 * block + bit, keep)):
                out[at, block] = kept[at, tile] + got[at, tile]


def third_kernel(group, kept, got, send, keep):
    one, two, _ = bits()
    bit = one if group else two

    @pl.loop(0, COUNT, unroll=4)
    def _(at):
        send[at] = kept[at, 1 - bit] + got[at, 1 - bit]
        keep[at] = kept[at, bit] + got[at, bit]


def slots_kernel(mom_ref, *outs):
    y = lax.axis_index("y")
    for step, out in enumerate(outs, start=1):
        out[...] = mom_ref[jnp.minimum((y + step) % 4, CAP - 1)]


def pack_kernel(target_ref, a_ref, got_a_ref, b_ref, got_b_ref, out_ref):
    for layer in range(L):
        for head in range(HEADS):
            where = target_ref[layer * HEADS + head]
            at = layer * SIZE + head % SIZE
            kept, got = (b_ref, got_b_ref) if head >= SIZE else (a_ref, got_a_ref)
            out_ref[where] = kept[at] + got[at]


def halves(value):
    high = value.astype(bf16)
    return high, (value - high.astype(f32)).astype(bf16)


def times(left, right, transposed):
    dims = (((1,), (1 if transposed else 0,)), ((), ()))

    def dot(a, b):
        return lax.dot_general(a, b, dims, preferred_element_type=f32)

    (lh, ll), (rh, rl) = left, right
    return dot(lh, rh) + (dot(lh, rl) + dot(ll, rh))


def newton(advance):
    norm = jnp.sqrt(jnp.sum(advance * advance))
    iterate = advance / (norm + norm_epsilon)
    for _ in range(ITERS):
        parts = halves(iterate)
        gram = times(parts, parts, True)
        gram_parts = halves(gram)
        poly = quintic_b * gram + quintic_c * times(gram_parts, gram_parts, False)
        iterate = quintic_a * iterate + times(halves(poly), parts, False)
    return iterate


def work_kernel(target_ref, got_ref, held_ref, mom1_ref, mom2_ref, mom3_ref, out_ref, own_ref, new1_ref, new2_ref, new3_ref, fresh, adv):
    y = lax.axis_index("y")
    me = y * OWNERS + (lax.axis_index("z") * 4 + lax.axis_index("x")) * 2 + lax.axis_index("core")
    live = jnp.max(jnp.where(target_ref[...] == me, 1, 0)) > 0
    for step, mom_ref in enumerate((None, mom1_ref, mom2_ref, mom3_ref)):
        block = (y + 4 - step) % 4
        for x, (one, two) in enumerate(((0, 0), (1, 0), (1, 1), (0, 1))):
            lanes = slice(two * 128, (two + 1) * 128)
            for core in range(2):
                for three in range(2):
                    tile = 4 * core + 2 * one + three
                    parts = [got_ref[block * 64 + (z * 4 + x) * 2 + core] for z in range(three, 8, 2)]
                    g = jnp.where(live, (parts[0] + parts[1]) + (parts[2] + parts[3]), 0.0)
                    if mom_ref is None:
                        mom = held_ref[jnp.minimum(y, CAP - 1), tile * 8 : tile * 8 + 8, lanes]
                    else:
                        mom = mom_ref[tile * 8 : tile * 8 + 8, lanes]
                    new = jnp.where(live, momentum_beta * mom + g, 0.0)
                    rows = rows_of(block * 8 + tile, 8)
                    fresh[rows, lanes] = new
                    adv[rows, lanes] = g + momentum_beta * new
    for step, out in enumerate((own_ref, new1_ref, new2_ref, new3_ref)):
        out[...] = fresh[rows_of((y + step) % 4, 64), :]
    ortho = newton(adv[...])
    for half in range(2):
        out_ref[pl.ds(half, RANK, stride=2), :] = ortho[:, half * 128 : (half + 1) * 128]


def finish_kernel(target_ref, got_ref, weights_ref, own_ref, new1_ref, new2_ref, new3_ref, mom_ref, step_ref, new_ref):
    y = lax.axis_index("y")
    for step, ref in enumerate((own_ref, new1_ref, new2_ref, new3_ref)):
        slot = (y + 4 - step) % 4

        @pl.when(slot < CAP)
        def _(slot=slot, ref=ref):
            mom_ref[slot] = ref[...]

    scale = rms_factor * math.sqrt(max(RANK, COLS))
    for layer in range(L):
        for head in range(HEADS):
            where = target_ref[layer * HEADS + head]
            lanes = slice(head * COLS, (head + 1) * COLS)
            held = weights_ref[layer, :, lanes]
            step = scale * got_ref[pl.ds(where, 1), 0, :] + decay_rate * held
            step_ref[layer, :, lanes] = step
            new_ref[layer, :, lanes] = held - learn_rate * step


def shape(*dims, dtype=f32):
    return jax.ShapeDtypeStruct(dims, dtype)


def call(kernel, outs, ins, scratch=(), flops=0, moved=1 << 22):
    many = isinstance(outs, tuple)
    out_spec = pl.BlockSpec(memory_space=pltpu.VMEM)
    return pl.pallas_call(
        kernel,
        out_shape=outs,
        in_specs=[pl.BlockSpec(memory_space=pltpu.SMEM if kind == "s" else pltpu.VMEM) for kind in ins],
        out_specs=tuple(out_spec for _ in outs) if many else out_spec,
        scratch_shapes=[pltpu.VMEM(dims, f32) for dims in scratch],
        compiler_params=params(),
        cost_estimate=pl.CostEstimate(flops=flops, bytes_accessed=moved, transcendentals=0),
        name=getattr(kernel, "func", kernel).__name__.removesuffix("_kernel"),
    )


def rows_of_heads(gradient, first, size, mine):
    return pl.pallas_call(
        functools.partial(rows_kernel, first, size, mine),
        out_shape=shape(L, 32, size * COLS, dtype=bf16),
        in_specs=[pl.BlockSpec(memory_space=pltpu.HBM)],
        out_specs=pl.BlockSpec(memory_space=pltpu.VMEM),
        scratch_shapes=[pltpu.SemaphoreType.DMA((L,))],
        compiler_params=params(),
        cost_estimate=pl.CostEstimate(flops=0, bytes_accessed=1 << 22, transcendentals=0),
        name="own" if mine else "cross",
    )(pltpu.with_memory_space_constraint(gradient, pltpu.HBM))


def route(moves):
    pairs = []
    for z in range(8):
        for x in range(4):
            for core, move in enumerate(moves):
                to_z, to_x = move(z, x)
                pairs.append(((z * 4 + x) * 2 + core, (to_z * 4 + to_x) * 2 + core))
    return pairs


def near(z, x):
    return z, x ^ 1


def far(z, x):
    return z, 3 - x


def pair(z, x):
    return z ^ 1, x


def link(z, x):
    return (z + 1 if z % 2 else z - 1) % 8, x


ROUTES = (
    (route((near, pair)), route((pair, near)), route((far, far))),
    (route((far, link)), route((link, far)), route((near, near))),
)


def along_y(values):
    return [
        lax.ppermute(value, "y", [(i, (i + step) % 4) for i in range(4)]) for step, value in enumerate(values, start=1)
    ]


def on_device(gradient, momentum, weights, table):
    target = targets(table)
    local = gradient[0]

    groups = range(2)
    dp = ("z", "x", "core")
    crossed = [lax.ppermute(rows_of_heads(local, group * SIZE, SIZE, False), "core", [(0, 1), (1, 0)]) for group in groups]
    own = [rows_of_heads(local, group * SIZE, SIZE, True) for group in groups]
    parts = [(own[group], crossed[group]) for group in groups]
    for step, (kernel, dims) in enumerate(((first_kernel, (4, 8, 128)), (second_kernel, (2, 8, 128)), (third_kernel, (8, 128)))):
        pieces = [call(functools.partial(kernel, group), (shape(COUNT, *dims),) * 2, "vv")(*parts[group]) for group in groups]
        parts = [(keep, lax.ppermute(send, dp, ROUTES[group][step])) for group, (send, keep) in enumerate(pieces)]
    moms = along_y(call(slots_kernel, (shape(64, COLS),) * 3, "v")(momentum[0]))

    outgoing = call(pack_kernel, shape(DEVICES, 8, 128), "svvvv")(target, *parts[0], *parts[1])
    got = lax.all_to_all(outgoing, ALL, 0, 0, tiled=True)
    outs = (shape(2 * RANK, 128),) + (shape(64, COLS),) * 4
    ortho, fresh, *news = call(work_kernel, outs, "vvvvvv", [(RANK, COLS), (RANK, COLS)], 15 * 3 * 2 * 256**3)(
        target.reshape(1, MATS), got, momentum[0], *moms
    )
    returned = lax.all_to_all(ortho.reshape(DEVICES, 1, COLS), ALL, 0, 0, tiled=True)
    news = along_y(news)
    outs = (shape(CAP, 64, COLS), shape(L, 1, HEADS * COLS), shape(L, 1, HEADS * COLS))
    new_momentum, step_update, new_weights = call(finish_kernel, outs, "svvvvvv")(target, returned, weights, fresh, *news)
    return new_momentum[None], step_update, new_weights


def solution(mesh):
    fine = Mesh(mesh.devices.reshape(8, 4, 2, 4), ("z", "x", "core", "y"))
    dp = ("z", "x", "core")
    return jax.shard_map(
        on_device,
        mesh=fine,
        in_specs=(
            P(dp, None, "y", None),
            P(dp, None, "y", None),
            P(None, ("y",) + dp, None),
            P(),
        ),
        out_specs=(
            P(dp, None, "y", None),
            P(None, ("y",) + dp, None),
            P(None, ("y",) + dp, None),
        ),
        check_vma=False,
    )
```

```python
import functools
import math

import jax
import jax.numpy as jnp
from jax import lax
from jax.experimental import pallas as pl
from jax.experimental.pallas import tpu as pltpu
from jax.sharding import Mesh, PartitionSpec as P

HEADS = 64
RANK = 256
COLS = 256
L = 2
ITERS = 5
MATS = L * HEADS
CAP = 3
SIZES = (16, 16, 16, 16)
KINDS = (0, 1, 0, 1)
FIRST = tuple(sum(SIZES[:group]) for group in range(len(SIZES)))
OWNERS = 64
DEVICES = 256
ALL = ("y", "z", "x", "core")

quintic_a = 3.4445
quintic_b = -4.775
quintic_c = 2.0315
momentum_beta = 0.95
learn_rate = 0.02
decay_rate = 0.1
rms_factor = 0.2
norm_epsilon = 1e-07
VMEM_LIMIT = 32 * 1024 * 1024

f32 = jnp.float32
bf16 = jnp.bfloat16


def targets(table):
    owners = table[:, 0]
    index = jnp.arange(MATS, dtype=jnp.int32)
    before = (owners[:, None] == owners[None, :]) & (index[:, None] < index[None, :])
    slots = jnp.sum(before.astype(jnp.int32), axis=0)
    return owners, slots


def params():
    return pltpu.CompilerParams(vmem_limit_bytes=VMEM_LIMIT)


def lanes_of(head, half):
    return pl.ds(pl.multiple_of(head * COLS + half * 128, 128), 128)


def rows_of(block, size):
    return pl.ds(pl.multiple_of(block * size, size), size)


def bits():
    x = lax.axis_index("x")
    second = x // 2
    return (x + second) % 2, second, lax.axis_index("z") % 2


def middle_bit(kind):
    one, two, three = bits()
    return jnp.where(lax.axis_index("core") == 0, three, two if kind else one)


def rows_kernel(mine, grad_ref, *refs):
    *outs, sems = refs
    core = lax.axis_index("core")
    rows = rows_of(core if mine else 1 - core, 32)
    copies = []
    for group, out in enumerate(outs):
        lanes = slice(FIRST[group] * COLS, (FIRST[group] + SIZES[group]) * COLS)
        for layer in range(L):
            copies.append(pltpu.make_async_copy(grad_ref.at[layer, rows, lanes], out.at[layer], sems.at[group, layer]))
    for copy in copies:
        copy.start()
    for copy in copies:
        copy.wait()


def total(own_ref, got_ref, layer, rows, lanes):
    return own_ref[layer, rows, lanes].astype(f32) + got_ref[layer, rows, lanes].astype(f32)


def first_kernel(kind, size, own_ref, got_ref, send, keep):
    one, two, three = bits()

    @pl.when(lax.axis_index("core") == 0)
    def _():
        @pl.loop(0, size, unroll=2)
        def _(head):
            for layer in range(L):
                at = layer * size + head
                for value, out in ((1 - (two if kind else one), send), ((two if kind else one), keep)):
                    for block in range(2):
                        if kind:
                            both = total(own_ref, got_ref, layer, slice(block * 16, block * 16 + 16), lanes_of(head, value))
                        else:
                            both = total(own_ref, got_ref, layer, rows_of(value, 16), lanes_of(head, block))
                        out[at, 2 * block] = both[:8]
                        out[at, 2 * block + 1] = both[8:]

    @pl.when(lax.axis_index("core") == 1)
    def _():
        @pl.loop(0, size, unroll=2)
        def _(head):
            for layer in range(L):
                at = layer * size + head
                for row in range(2):
                    for lane in range(2):
                        both = total(own_ref, got_ref, layer, slice(row * 16, row * 16 + 16), lanes_of(head, lane))
                        tile = 2 * row + lane if kind else 2 * lane + row
                        send[at, tile] = jnp.where(three == 0, both[8:], both[:8])
                        keep[at, tile] = jnp.where(three == 0, both[:8], both[8:])


def second_kernel(kind, size, kept, got, send, keep):
    bit = middle_bit(kind)

    @pl.loop(0, L * size, unroll=4)
    def _(at):
        for block in range(2):
            for tile, out in ((2 * block + 1 - bit, send), (2 * block + bit, keep)):
                out[at, block] = kept[at, tile] + got[at, tile]


def third_kernel(kind, size, kept, got, send, keep):
    one, two, _ = bits()
    bit = one if kind else two

    @pl.loop(0, L * size, unroll=4)
    def _(at):
        send[at] = kept[at, 1 - bit] + got[at, 1 - bit]
        keep[at] = kept[at, bit] + got[at, bit]


def pack_kernel(place_ref, *refs):
    out_ref = refs[-1]
    for group, size in enumerate(SIZES):
        for layer in range(L):
            for head in range(size):
                where = place_ref[layer * HEADS + FIRST[group] + head]
                out_ref[where] = refs[2 * group][layer * size + head] + refs[2 * group + 1][layer * size + head]


def halves(value):
    high = value.astype(bf16)
    return high, (value - high.astype(f32)).astype(bf16)


def times(left, right, transposed):
    dims = (((1,), (1 if transposed else 0,)), ((), ()))

    def dot(a, b):
        return lax.dot_general(a, b, dims, preferred_element_type=f32)

    (lh, ll), (rh, rl) = left, right
    return dot(lh, rh) + (dot(lh, rl) + dot(ll, rh))


def newton(advance):
    norm = jnp.sqrt(jnp.sum(advance * advance))
    iterate = advance / (norm + norm_epsilon)
    for _ in range(ITERS):
        parts = halves(iterate)
        gram = times(parts, parts, True)
        gram_parts = halves(gram)
        poly = quintic_b * gram + quintic_c * times(gram_parts, gram_parts, False)
        iterate = quintic_a * iterate + times(halves(poly), parts, False)
    return iterate


def update_kernel(place_ref, got_ref, mom_ref, fresh_ref, own_ref, send1_ref, send2_ref, send3_ref, adv):
    me = (lax.axis_index("z") * 4 + lax.axis_index("x")) * 2 + lax.axis_index("core")
    for slot in range(CAP):
        live = jnp.max(jnp.where(place_ref[...] == me * CAP + slot, 1, 0)) > 0
        for x, (one, two) in enumerate(((0, 0), (1, 0), (1, 1), (0, 1))):
            lanes = slice(two * 128, (two + 1) * 128)
            for core in range(2):
                for three in range(2):
                    rows = slice((4 * core + 2 * one + three) * 8, (4 * core + 2 * one + three + 1) * 8)
                    parts = [got_ref[((z * 4 + x) * 2 + core) * CAP + slot] for z in range(three, 8, 2)]
                    g = jnp.where(live, (parts[0] + parts[1]) + (parts[2] + parts[3]), 0.0)
                    new = jnp.where(live, momentum_beta * mom_ref[slot, rows, lanes] + g, 0.0)
                    fresh_ref[slot, rows, lanes] = new
                    adv[slot, rows, lanes] = g + momentum_beta * new
    y = lax.axis_index("y")
    for step, out in enumerate((own_ref, send1_ref, send2_ref, send3_ref)):
        out[...] = adv[jnp.minimum((y + step) % 4, CAP - 1)]


def work_kernel(own_ref, got1_ref, got2_ref, got3_ref, out_ref, adv):
    y = lax.axis_index("y")
    for step, ref in enumerate((own_ref, got1_ref, got2_ref, got3_ref)):
        adv[rows_of((y + 4 - step) % 4, 64), :] = ref[...]
    ortho = newton(adv[...])
    for half in range(2):
        out_ref[pl.ds(half, RANK, stride=2), :] = ortho[:, half * 128 : (half + 1) * 128]


def finish_kernel(target_ref, got_ref, weights_ref, step_ref, new_ref, gathered):
    for at in range(MATS):
        gathered[2 * at : 2 * at + 2, :] = got_ref[pl.ds(2 * target_ref[at], 2), :]
    scale = rms_factor * math.sqrt(max(RANK, COLS))
    step = scale * gathered[...] + decay_rate * weights_ref[...]
    step_ref[...] = step
    new_ref[...] = weights_ref[...] - learn_rate * step


def shape(*dims, dtype=f32):
    return jax.ShapeDtypeStruct(dims, dtype)


def call(kernel, outs, ins, scratch=(), flops=0, moved=1 << 10):
    many = isinstance(outs, tuple)
    out_spec = pl.BlockSpec(memory_space=pltpu.VMEM)
    return pl.pallas_call(
        kernel,
        out_shape=outs,
        in_specs=[pl.BlockSpec(memory_space=pltpu.SMEM if kind == "s" else pltpu.VMEM) for kind in ins],
        out_specs=tuple(out_spec for _ in outs) if many else out_spec,
        scratch_shapes=[pltpu.VMEM(dims, f32) for dims in scratch],
        compiler_params=params(),
        cost_estimate=pl.CostEstimate(flops=flops, bytes_accessed=moved, transcendentals=0),
        name=getattr(kernel, "func", kernel).__name__.removesuffix("_kernel"),
    )


def rows_of_heads(gradient, mine):
    return pl.pallas_call(
        functools.partial(rows_kernel, mine),
        out_shape=tuple(shape(L, 32, size * COLS, dtype=bf16) for size in SIZES),
        in_specs=[pl.BlockSpec(memory_space=pltpu.HBM)],
        out_specs=tuple(pl.BlockSpec(memory_space=pltpu.VMEM) for _ in SIZES),
        scratch_shapes=[pltpu.SemaphoreType.DMA((len(SIZES), L))],
        compiler_params=params(),
        cost_estimate=pl.CostEstimate(flops=0, bytes_accessed=1 << 10, transcendentals=0),
        name="own" if mine else "cross",
    )(pltpu.with_memory_space_constraint(gradient, pltpu.HBM))


def route(moves):
    pairs = []
    for z in range(8):
        for x in range(4):
            for core, move in enumerate(moves):
                to_z, to_x = move(z, x)
                pairs.append(((z * 4 + x) * 2 + core, (to_z * 4 + to_x) * 2 + core))
    return pairs


def near(z, x):
    return z, x ^ 1


def far(z, x):
    return z, 3 - x


def pair(z, x):
    return z ^ 1, x


def link(z, x):
    return (z + 1 if z % 2 else z - 1) % 8, x


ROUTES = (
    (route((near, pair)), route((pair, near)), route((far, far))),
    (route((far, link)), route((link, far)), route((near, near))),
)


def along_y(values):
    return [
        lax.ppermute(value, "y", [(i, (i + step) % 4) for i in range(4)]) for step, value in enumerate(values, start=1)
    ]


def on_device(gradient, momentum, weights, table):
    owners, slots = targets(table)
    local = gradient[0]

    dp = ("z", "x", "core")
    crossed = [lax.ppermute(rows, "core", [(0, 1), (1, 0)]) for rows in rows_of_heads(local, False)]
    parts = list(zip(rows_of_heads(local, True), crossed))
    for step, (kernel, dims) in enumerate(((first_kernel, (4, 8, 128)), (second_kernel, (2, 8, 128)), (third_kernel, (8, 128)))):
        for group, (kind, size) in enumerate(zip(KINDS, SIZES)):
            send, keep = call(functools.partial(kernel, kind, size), (shape(L * size, *dims),) * 2, "vv")(*parts[group])
            parts[group] = keep, lax.ppermute(send, dp, ROUTES[kind][step])

    place = owners * CAP + slots
    outgoing = call(pack_kernel, shape(OWNERS * CAP, 8, 128), "s" + "vv" * len(SIZES))(place, *sum(parts, ()))
    got = lax.all_to_all(outgoing, dp, 0, 0, tiled=True)
    outs = (shape(CAP, 64, COLS),) + (shape(64, COLS),) * 4
    fresh, mine, *sends = call(update_kernel, outs, "vvv", [(CAP, 64, COLS)])(place.reshape(1, MATS), got, momentum[0])
    ortho = call(work_kernel, shape(2 * RANK, 128), "vvvv", [(RANK, COLS)], 15 * 3 * 2 * 256**3)(mine, *along_y(sends))
    returned = lax.all_to_all(ortho.reshape(DEVICES, 1, COLS), ALL, 0, 0, tiled=True).reshape(2 * DEVICES, 128)
    step_update, new_weights = call(finish_kernel, (shape(2 * MATS, 128),) * 2, "svv", [(2 * MATS, 128)])(
        slots * OWNERS + owners, returned, weights.reshape(2 * MATS, 128)
    )
    return fresh[None], step_update.reshape(weights.shape), new_weights.reshape(weights.shape)


def solution(mesh):
    fine = Mesh(mesh.devices.reshape(8, 4, 2, 4), ("z", "x", "core", "y"))
    dp = ("z", "x", "core")
    return jax.shard_map(
        on_device,
        mesh=fine,
        in_specs=(
            P(dp, None, "y", None),
            P(dp, None, "y", None),
            P(None, ("y",) + dp, None),
            P(),
        ),
        out_specs=(
            P(dp, None, "y", None),
            P(None, ("y",) + dp, None),
            P(None, ("y",) + dp, None),
        ),
        check_vma=False,
    )
```

```python
import functools
import math

import jax
import jax.numpy as jnp
from jax import lax
from jax.experimental import pallas as pl
from jax.experimental.pallas import tpu as pltpu
from jax.sharding import Mesh, PartitionSpec as P

HEADS = 64
RANK = 256
COLS = 256
L = 2
ITERS = 5
MATS = L * HEADS
CAP = 3
SIZES = (22, 22, 10, 10)
KINDS = (0, 1, 0, 1)
FIRST = tuple(sum(SIZES[:group]) for group in range(len(SIZES)))
OWNERS = 64
DEVICES = 256
ALL = ("y", "z", "x", "core")

quintic_a = 3.4445
quintic_b = -4.775
quintic_c = 2.0315
momentum_beta = 0.95
learn_rate = 0.02
decay_rate = 0.1
rms_factor = 0.2
norm_epsilon = 1e-07
VMEM_LIMIT = 32 * 1024 * 1024

f32 = jnp.float32
bf16 = jnp.bfloat16


def targets(table):
    owners = table[:, 0]
    index = jnp.arange(MATS, dtype=jnp.int32)
    before = (owners[:, None] == owners[None, :]) & (index[:, None] < index[None, :])
    slots = jnp.sum(before.astype(jnp.int32), axis=0)
    return owners, slots


def params():
    return pltpu.CompilerParams(vmem_limit_bytes=VMEM_LIMIT)


def lanes_of(head, half):
    return pl.ds(pl.multiple_of(head * COLS + half * 128, 128), 128)


def rows_of(block, size):
    return pl.ds(pl.multiple_of(block * size, size), size)


def bits():
    x = lax.axis_index("x")
    second = x // 2
    return (x + second) % 2, second, lax.axis_index("z") % 2


def middle_bit(kind):
    one, two, three = bits()
    return jnp.where(lax.axis_index("core") == 0, three, two if kind else one)


def rows_kernel(mine, grad_ref, *refs):
    *outs, sems = refs
    core = lax.axis_index("core")
    rows = rows_of(core if mine else 1 - core, 32)
    copies = []
    for group, out in enumerate(outs):
        lanes = slice(FIRST[group] * COLS, (FIRST[group] + SIZES[group]) * COLS)
        for layer in range(L):
            copies.append(pltpu.make_async_copy(grad_ref.at[layer, rows, lanes], out.at[layer], sems.at[group, layer]))
    for copy in copies:
        copy.start()
    for copy in copies:
        copy.wait()


def total(own_ref, got_ref, layer, rows, lanes):
    return own_ref[layer, rows, lanes].astype(f32) + got_ref[layer, rows, lanes].astype(f32)


def first_kernel(kind, size, own_ref, got_ref, send, keep):
    one, two, three = bits()

    @pl.when(lax.axis_index("core") == 0)
    def _():
        @pl.loop(0, size, unroll=2)
        def _(head):
            for layer in range(L):
                at = layer * size + head
                for value, out in ((1 - (two if kind else one), send), ((two if kind else one), keep)):
                    for block in range(2):
                        if kind:
                            both = total(own_ref, got_ref, layer, slice(block * 16, block * 16 + 16), lanes_of(head, value))
                        else:
                            both = total(own_ref, got_ref, layer, rows_of(value, 16), lanes_of(head, block))
                        out[at, 2 * block] = both[:8]
                        out[at, 2 * block + 1] = both[8:]

    @pl.when(lax.axis_index("core") == 1)
    def _():
        @pl.loop(0, size, unroll=2)
        def _(head):
            for layer in range(L):
                at = layer * size + head
                for row in range(2):
                    for lane in range(2):
                        both = total(own_ref, got_ref, layer, slice(row * 16, row * 16 + 16), lanes_of(head, lane))
                        tile = 2 * row + lane if kind else 2 * lane + row
                        send[at, tile] = jnp.where(three == 0, both[8:], both[:8])
                        keep[at, tile] = jnp.where(three == 0, both[:8], both[8:])


def second_kernel(kind, size, kept, got, send, keep):
    bit = middle_bit(kind)

    @pl.loop(0, L * size, unroll=4)
    def _(at):
        for block in range(2):
            for tile, out in ((2 * block + 1 - bit, send), (2 * block + bit, keep)):
                out[at, block] = kept[at, tile] + got[at, tile]


def third_kernel(kind, *refs):
    send, keep = refs[-2:]
    one, two, _ = bits()
    bit = one if kind else two
    begin = 0
    for turn, count in enumerate(L * size for group, size in enumerate(SIZES) if KINDS[group] == kind):
        kept, got = refs[2 * turn : 2 * turn + 2]

        @pl.loop(0, count, unroll=4)
        def _(at, kept=kept, got=got, begin=begin):
            send[begin + at] = kept[at, 1 - bit] + got[at, 1 - bit]
            keep[begin + at] = kept[at, bit] + got[at, bit]

        begin += count


def pack_kernel(place_ref, a_ref, got_a_ref, b_ref, got_b_ref, out_ref):
    begin = [0, 0]
    for kind, first, size in zip(KINDS, FIRST, SIZES):
        kept, got = (b_ref, got_b_ref) if kind else (a_ref, got_a_ref)
        for layer in range(L):
            for head in range(size):
                at = begin[kind] + layer * size + head
                out_ref[place_ref[layer * HEADS + first + head]] = kept[at] + got[at]
        begin[kind] += L * size


def halves(value):
    high = value.astype(bf16)
    return high, (value - high.astype(f32)).astype(bf16)


def times(left, right, transposed):
    dims = (((1,), (1 if transposed else 0,)), ((), ()))

    def dot(a, b):
        return lax.dot_general(a, b, dims, preferred_element_type=f32)

    (lh, ll), (rh, rl) = left, right
    return dot(lh, rh) + (dot(lh, rl) + dot(ll, rh))


def newton(advance):
    norm = jnp.sqrt(jnp.sum(advance * advance))
    iterate = advance / (norm + norm_epsilon)
    for _ in range(ITERS):
        parts = halves(iterate)
        gram = times(parts, parts, True)
        gram_parts = halves(gram)
        poly = quintic_b * gram + quintic_c * times(gram_parts, gram_parts, False)
        iterate = quintic_a * iterate + times(halves(poly), parts, False)
    return iterate


def update_kernel(place_ref, got_ref, mom_ref, fresh_ref, own_ref, send1_ref, send2_ref, send3_ref, adv):
    me = (lax.axis_index("z") * 4 + lax.axis_index("x")) * 2 + lax.axis_index("core")
    for slot in range(CAP):
        live = jnp.max(jnp.where(place_ref[...] == me * CAP + slot, 1, 0)) > 0
        for x, (one, two) in enumerate(((0, 0), (1, 0), (1, 1), (0, 1))):
            lanes = slice(two * 128, (two + 1) * 128)
            for core in range(2):
                for three in range(2):
                    rows = slice((4 * core + 2 * one + three) * 8, (4 * core + 2 * one + three + 1) * 8)
                    parts = [got_ref[((z * 4 + x) * 2 + core) * CAP + slot] for z in range(three, 8, 2)]
                    g = jnp.where(live, (parts[0] + parts[1]) + (parts[2] + parts[3]), 0.0)
                    new = jnp.where(live, momentum_beta * mom_ref[slot, rows, lanes] + g, 0.0)
                    fresh_ref[slot, rows, lanes] = new
                    adv[slot, rows, lanes] = g + momentum_beta * new
    y = lax.axis_index("y")
    for step, out in enumerate((own_ref, send1_ref, send2_ref, send3_ref)):
        out[...] = adv[jnp.minimum((y + step) % 4, CAP - 1)]


def work_kernel(own_ref, got1_ref, got2_ref, got3_ref, out_ref, adv):
    y = lax.axis_index("y")
    for step, ref in enumerate((own_ref, got1_ref, got2_ref, got3_ref)):
        adv[rows_of((y + 4 - step) % 4, 64), :] = ref[...]
    ortho = newton(adv[...])
    for half in range(2):
        out_ref[pl.ds(half, RANK, stride=2), :] = ortho[:, half * 128 : (half + 1) * 128]


def finish_kernel(target_ref, got_ref, weights_ref, step_ref, new_ref, gathered):
    for at in range(MATS):
        gathered[2 * at : 2 * at + 2, :] = got_ref[pl.ds(2 * target_ref[at], 2), :]
    scale = rms_factor * math.sqrt(max(RANK, COLS))
    step = scale * gathered[...] + decay_rate * weights_ref[...]
    step_ref[...] = step
    new_ref[...] = weights_ref[...] - learn_rate * step


def shape(*dims, dtype=f32):
    return jax.ShapeDtypeStruct(dims, dtype)


def call(kernel, outs, ins, scratch=(), flops=0, moved=1 << 10):
    many = isinstance(outs, tuple)
    out_spec = pl.BlockSpec(memory_space=pltpu.VMEM)
    return pl.pallas_call(
        kernel,
        out_shape=outs,
        in_specs=[pl.BlockSpec(memory_space=pltpu.SMEM if kind == "s" else pltpu.VMEM) for kind in ins],
        out_specs=tuple(out_spec for _ in outs) if many else out_spec,
        scratch_shapes=[pltpu.VMEM(dims, f32) for dims in scratch],
        compiler_params=params(),
        cost_estimate=pl.CostEstimate(flops=flops, bytes_accessed=moved, transcendentals=0),
        name=getattr(kernel, "func", kernel).__name__.removesuffix("_kernel"),
    )


def rows_of_heads(gradient, mine):
    return pl.pallas_call(
        functools.partial(rows_kernel, mine),
        out_shape=tuple(shape(L, 32, size * COLS, dtype=bf16) for size in SIZES),
        in_specs=[pl.BlockSpec(memory_space=pltpu.HBM)],
        out_specs=tuple(pl.BlockSpec(memory_space=pltpu.VMEM) for _ in SIZES),
        scratch_shapes=[pltpu.SemaphoreType.DMA((len(SIZES), L))],
        compiler_params=params(),
        cost_estimate=pl.CostEstimate(flops=0, bytes_accessed=1 << 10, transcendentals=0),
        name="own" if mine else "cross",
    )(pltpu.with_memory_space_constraint(gradient, pltpu.HBM))


def route(moves):
    pairs = []
    for z in range(8):
        for x in range(4):
            for core, move in enumerate(moves):
                to_z, to_x = move(z, x)
                pairs.append(((z * 4 + x) * 2 + core, (to_z * 4 + to_x) * 2 + core))
    return pairs


def near(z, x):
    return z, x ^ 1


def far(z, x):
    return z, 3 - x


def pair(z, x):
    return z ^ 1, x


def link(z, x):
    return (z + 1 if z % 2 else z - 1) % 8, x


ROUTES = (
    (route((near, pair)), route((pair, near)), route((far, far))),
    (route((far, link)), route((link, far)), route((near, near))),
)


def along_y(values):
    return [
        lax.ppermute(value, "y", [(i, (i + step) % 4) for i in range(4)]) for step, value in enumerate(values, start=1)
    ]


def on_device(gradient, momentum, weights, table):
    owners, slots = targets(table)
    local = gradient[0]

    dp = ("z", "x", "core")
    crossed = [lax.ppermute(rows, "core", [(0, 1), (1, 0)]) for rows in rows_of_heads(local, False)]
    parts = list(zip(rows_of_heads(local, True), crossed))
    for step, (kernel, dims) in enumerate(((first_kernel, (4, 8, 128)), (second_kernel, (2, 8, 128)))):
        for group, (kind, size) in enumerate(zip(KINDS, SIZES)):
            send, keep = call(functools.partial(kernel, kind, size), (shape(L * size, *dims),) * 2, "vv")(*parts[group])
            parts[group] = keep, lax.ppermute(send, dp, ROUTES[kind][step])
    last = ()
    for kind in range(2):
        held = sum((part for part, is_kind in zip(parts, KINDS) if is_kind == kind), ())
        outs = (shape(sum(part.shape[0] for part in held[::2]), 8, 128),) * 2
        send, keep = call(functools.partial(third_kernel, kind), outs, "v" * len(held))(*held)
        last += keep, lax.ppermute(send, dp, ROUTES[kind][2])

    place = owners * CAP + slots
    outgoing = call(pack_kernel, shape(OWNERS * CAP, 8, 128), "svvvv")(place, *last)
    got = lax.all_to_all(outgoing, dp, 0, 0, tiled=True)
    outs = (shape(CAP, 64, COLS),) + (shape(64, COLS),) * 4
    fresh, mine, *sends = call(update_kernel, outs, "vvv", [(CAP, 64, COLS)])(place.reshape(1, MATS), got, momentum[0])
    ortho = call(work_kernel, shape(2 * RANK, 128), "vvvv", [(RANK, COLS)], 15 * 3 * 2 * 256**3)(mine, *along_y(sends))
    returned = lax.all_to_all(ortho.reshape(DEVICES, 1, COLS), ALL, 0, 0, tiled=True).reshape(2 * DEVICES, 128)
    step_update, new_weights = call(finish_kernel, (shape(2 * MATS, 128),) * 2, "svv", [(2 * MATS, 128)])(
        slots * OWNERS + owners, returned, weights.reshape(2 * MATS, 128)
    )
    return fresh[None], step_update.reshape(weights.shape), new_weights.reshape(weights.shape)


def solution(mesh):
    fine = Mesh(mesh.devices.reshape(8, 4, 2, 4), ("z", "x", "core", "y"))
    dp = ("z", "x", "core")
    return jax.shard_map(
        on_device,
        mesh=fine,
        in_specs=(
            P(dp, None, "y", None),
            P(dp, None, "y", None),
            P(None, ("y",) + dp, None),
            P(),
        ),
        out_specs=(
            P(dp, None, "y", None),
            P(None, ("y",) + dp, None),
            P(None, ("y",) + dp, None),
        ),
        check_vma=False,
    )
```

```python
import functools
import math

import jax
import jax.numpy as jnp
from jax import lax
from jax.experimental import pallas as pl
from jax.experimental.pallas import tpu as pltpu
from jax.sharding import Mesh, PartitionSpec as P

HEADS = 64
RANK = 256
COLS = 256
L = 2
ITERS = 5
MATS = L * HEADS
CAP = 3
SIZES = (22, 22, 10, 10)
KINDS = (0, 1, 0, 1)
FIRST = tuple(sum(SIZES[:group]) for group in range(len(SIZES)))
OWNERS = 64
DEVICES = 256
ALL = ("y", "z", "x", "core")

quintic_a = 3.4445
quintic_b = -4.775
quintic_c = 2.0315
momentum_beta = 0.95
learn_rate = 0.02
decay_rate = 0.1
rms_factor = 0.2
norm_epsilon = 1e-07
VMEM_LIMIT = 32 * 1024 * 1024

f32 = jnp.float32
bf16 = jnp.bfloat16


def targets(table):
    owners = table[:, 0]
    index = jnp.arange(MATS, dtype=jnp.int32)
    before = (owners[:, None] == owners[None, :]) & (index[:, None] < index[None, :])
    slots = jnp.sum(before.astype(jnp.int32), axis=0)
    return owners, slots


def params():
    return pltpu.CompilerParams(vmem_limit_bytes=VMEM_LIMIT)


def lanes_of(head, half):
    return pl.ds(pl.multiple_of(head * COLS + half * 128, 128), 128)


def rows_of(block, size):
    return pl.ds(pl.multiple_of(block * size, size), size)


def bits():
    x = lax.axis_index("x")
    second = x // 2
    return (x + second) % 2, second, lax.axis_index("z") % 2


def middle_bit(kind):
    one, two, three = bits()
    return jnp.where(lax.axis_index("core") == 0, three, two if kind else one)


def rows_kernel(mine, groups, grad_ref, *refs):
    *outs, sems = refs
    core = lax.axis_index("core")
    rows = rows_of(core if mine else 1 - core, 32)
    copies = []
    for turn, (group, out) in enumerate(zip(groups, outs)):
        lanes = slice(FIRST[group] * COLS, (FIRST[group] + SIZES[group]) * COLS)
        for layer in range(L):
            copies.append(pltpu.make_async_copy(grad_ref.at[layer, rows, lanes], out.at[layer], sems.at[turn, layer]))
    for copy in copies:
        copy.start()
    for copy in copies:
        copy.wait()


def total(own_ref, got_ref, layer, rows, lanes):
    return own_ref[layer, rows, lanes].astype(f32) + got_ref[layer, rows, lanes].astype(f32)


def first_kernel(kind, size, own_ref, got_ref, send, keep):
    one, two, three = bits()

    @pl.when(lax.axis_index("core") == 0)
    def _():
        @pl.loop(0, size, unroll=2)
        def _(head):
            for layer in range(L):
                at = layer * size + head
                for value, out in ((1 - (two if kind else one), send), ((two if kind else one), keep)):
                    for block in range(2):
                        if kind:
                            both = total(own_ref, got_ref, layer, slice(block * 16, block * 16 + 16), lanes_of(head, value))
                        else:
                            both = total(own_ref, got_ref, layer, rows_of(value, 16), lanes_of(head, block))
                        out[at, 2 * block] = both[:8]
                        out[at, 2 * block + 1] = both[8:]

    @pl.when(lax.axis_index("core") == 1)
    def _():
        @pl.loop(0, size, unroll=2)
        def _(head):
            for layer in range(L):
                at = layer * size + head
                for row in range(2):
                    for lane in range(2):
                        both = total(own_ref, got_ref, layer, slice(row * 16, row * 16 + 16), lanes_of(head, lane))
                        tile = 2 * row + lane if kind else 2 * lane + row
                        send[at, tile] = jnp.where(three == 0, both[8:], both[:8])
                        keep[at, tile] = jnp.where(three == 0, both[:8], both[8:])


def second_kernel(kind, size, kept, got, send, keep):
    bit = middle_bit(kind)

    @pl.loop(0, L * size, unroll=4)
    def _(at):
        for block in range(2):
            for tile, out in ((2 * block + 1 - bit, send), (2 * block + bit, keep)):
                out[at, block] = kept[at, tile] + got[at, tile]


def third_kernel(kind, *refs):
    send, keep = refs[-2:]
    one, two, _ = bits()
    bit = one if kind else two
    begin = 0
    for turn, count in enumerate(L * size for group, size in enumerate(SIZES) if KINDS[group] == kind):
        kept, got = refs[2 * turn : 2 * turn + 2]

        @pl.loop(0, count, unroll=4)
        def _(at, kept=kept, got=got, begin=begin):
            send[begin + at] = kept[at, 1 - bit] + got[at, 1 - bit]
            keep[begin + at] = kept[at, bit] + got[at, bit]

        begin += count


def pack_kernel(place_ref, a_ref, got_a_ref, b_ref, got_b_ref, out_ref):
    begin = [0, 0]
    for kind, first, size in zip(KINDS, FIRST, SIZES):
        kept, got = (b_ref, got_b_ref) if kind else (a_ref, got_a_ref)
        for layer in range(L):
            for head in range(size):
                at = begin[kind] + layer * size + head
                out_ref[place_ref[layer * HEADS + first + head]] = kept[at] + got[at]
        begin[kind] += L * size


def halves(value):
    high = value.astype(bf16)
    return high, (value - high.astype(f32)).astype(bf16)


def times(left, right, transposed):
    dims = (((1,), (1 if transposed else 0,)), ((), ()))

    def dot(a, b):
        return lax.dot_general(a, b, dims, preferred_element_type=f32)

    (lh, ll), (rh, rl) = left, right
    return dot(lh, rh) + (dot(lh, rl) + dot(ll, rh))


def newton(advance):
    norm = jnp.sqrt(jnp.sum(advance * advance))
    iterate = advance / (norm + norm_epsilon)
    for _ in range(ITERS):
        parts = halves(iterate)
        gram = times(parts, parts, True)
        gram_parts = halves(gram)
        poly = quintic_b * gram + quintic_c * times(gram_parts, gram_parts, False)
        iterate = quintic_a * iterate + times(halves(poly), parts, False)
    return iterate


def update_kernel(place_ref, got_ref, mom_ref, fresh_ref, own_ref, send1_ref, send2_ref, send3_ref, adv):
    me = (lax.axis_index("z") * 4 + lax.axis_index("x")) * 2 + lax.axis_index("core")
    for slot in range(CAP):
        live = jnp.max(jnp.where(place_ref[...] == me * CAP + slot, 1, 0)) > 0
        for x, (one, two) in enumerate(((0, 0), (1, 0), (1, 1), (0, 1))):
            lanes = slice(two * 128, (two + 1) * 128)
            for core in range(2):
                for three in range(2):
                    rows = slice((4 * core + 2 * one + three) * 8, (4 * core + 2 * one + three + 1) * 8)
                    parts = [got_ref[((z * 4 + x) * 2 + core) * CAP + slot] for z in range(three, 8, 2)]
                    g = jnp.where(live, (parts[0] + parts[1]) + (parts[2] + parts[3]), 0.0)
                    new = jnp.where(live, momentum_beta * mom_ref[slot, rows, lanes] + g, 0.0)
                    fresh_ref[slot, rows, lanes] = new
                    adv[slot, rows, lanes] = g + momentum_beta * new
    y = lax.axis_index("y")
    for step, out in enumerate((own_ref, send1_ref, send2_ref, send3_ref)):
        out[...] = adv[jnp.minimum((y + step) % 4, CAP - 1)]


def work_kernel(own_ref, got1_ref, got2_ref, got3_ref, out_ref, adv):
    y = lax.axis_index("y")
    for step, ref in enumerate((own_ref, got1_ref, got2_ref, got3_ref)):
        adv[rows_of((y + 4 - step) % 4, 64), :] = ref[...]
    ortho = newton(adv[...])
    for half in range(2):
        out_ref[pl.ds(half, RANK, stride=2), :] = ortho[:, half * 128 : (half + 1) * 128]


def finish_kernel(target_ref, got_ref, weights_ref, step_ref, new_ref, gathered):
    for at in range(MATS):
        gathered[2 * at : 2 * at + 2, :] = got_ref[pl.ds(2 * target_ref[at], 2), :]
    scale = rms_factor * math.sqrt(max(RANK, COLS))
    step = scale * gathered[...] + decay_rate * weights_ref[...]
    step_ref[...] = step
    new_ref[...] = weights_ref[...] - learn_rate * step


def shape(*dims, dtype=f32):
    return jax.ShapeDtypeStruct(dims, dtype)


def call(kernel, outs, ins, scratch=(), flops=0, moved=1 << 10):
    many = isinstance(outs, tuple)
    out_spec = pl.BlockSpec(memory_space=pltpu.VMEM)
    return pl.pallas_call(
        kernel,
        out_shape=outs,
        in_specs=[pl.BlockSpec(memory_space=pltpu.SMEM if kind == "s" else pltpu.VMEM) for kind in ins],
        out_specs=tuple(out_spec for _ in outs) if many else out_spec,
        scratch_shapes=[pltpu.VMEM(dims, f32) for dims in scratch],
        compiler_params=params(),
        cost_estimate=pl.CostEstimate(flops=flops, bytes_accessed=moved, transcendentals=0),
        name=getattr(kernel, "func", kernel).__name__.removesuffix("_kernel"),
    )


def rows_of_heads(gradient, mine, groups):
    return pl.pallas_call(
        functools.partial(rows_kernel, mine, groups),
        out_shape=tuple(shape(L, 32, SIZES[group] * COLS, dtype=bf16) for group in groups),
        in_specs=[pl.BlockSpec(memory_space=pltpu.HBM)],
        out_specs=tuple(pl.BlockSpec(memory_space=pltpu.VMEM) for _ in groups),
        scratch_shapes=[pltpu.SemaphoreType.DMA((len(groups), L))],
        compiler_params=params(),
        cost_estimate=pl.CostEstimate(flops=0, bytes_accessed=1 << 10, transcendentals=0),
        name="own" if mine else "cross",
    )(pltpu.with_memory_space_constraint(gradient, pltpu.HBM))


def route(moves):
    pairs = []
    for z in range(8):
        for x in range(4):
            for core, move in enumerate(moves):
                to_z, to_x = move(z, x)
                pairs.append(((z * 4 + x) * 2 + core, (to_z * 4 + to_x) * 2 + core))
    return pairs


def near(z, x):
    return z, x ^ 1


def far(z, x):
    return z, 3 - x


def pair(z, x):
    return z ^ 1, x


def link(z, x):
    return (z + 1 if z % 2 else z - 1) % 8, x


ROUTES = (
    (route((near, pair)), route((pair, near)), route((far, far))),
    (route((far, link)), route((link, far)), route((near, near))),
)


def along_y(values):
    one, two, three = values
    two = lax.ppermute(two, "y", [(i, (i + 2) % 4) for i in range(4)])
    one, three = (lax.ppermute(value, "y", [(i, (i + step) % 4) for i in range(4)]) for step, value in ((1, one), (3, three)))
    return one, two, three


def on_device(gradient, momentum, weights, table):
    owners, slots = targets(table)
    local = gradient[0]

    dp = ("z", "x", "core")
    crossed = sum((rows_of_heads(local, False, groups) for groups in ((0, 1), (2, 3))), ())
    crossed = [lax.ppermute(rows, "core", [(0, 1), (1, 0)]) for rows in crossed]
    parts = list(zip(sum((rows_of_heads(local, True, groups) for groups in ((0, 1), (2, 3))), ()), crossed))
    for step, (kernel, dims) in enumerate(((first_kernel, (4, 8, 128)), (second_kernel, (2, 8, 128)))):
        for group, (kind, size) in enumerate(zip(KINDS, SIZES)):
            send, keep = call(functools.partial(kernel, kind, size), (shape(L * size, *dims),) * 2, "vv")(*parts[group])
            parts[group] = keep, lax.ppermute(send, dp, ROUTES[kind][step])
    last = ()
    for kind in range(2):
        held = sum((part for part, is_kind in zip(parts, KINDS) if is_kind == kind), ())
        outs = (shape(sum(part.shape[0] for part in held[::2]), 8, 128),) * 2
        send, keep = call(functools.partial(third_kernel, kind), outs, "v" * len(held))(*held)
        last += keep, lax.ppermute(send, dp, ROUTES[kind][2])

    place = owners * CAP + slots
    outgoing = call(pack_kernel, shape(OWNERS * CAP, 8, 128), "svvvv")(place, *last)
    got = lax.all_to_all(outgoing, dp, 0, 0, tiled=True)
    outs = (shape(CAP, 64, COLS),) + (shape(64, COLS),) * 4
    fresh, mine, *sends = call(update_kernel, outs, "vvv", [(CAP, 64, COLS)])(place.reshape(1, MATS), got, momentum[0])
    ortho = call(work_kernel, shape(2 * RANK, 128), "vvvv", [(RANK, COLS)], 15 * 3 * 2 * 256**3)(mine, *along_y(sends))
    returned = lax.all_to_all(ortho.reshape(DEVICES, 1, COLS), ALL, 0, 0, tiled=True).reshape(2 * DEVICES, 128)
    step_update, new_weights = call(finish_kernel, (shape(2 * MATS, 128),) * 2, "svv", [(2 * MATS, 128)])(
        slots * OWNERS + owners, returned, weights.reshape(2 * MATS, 128)
    )
    return fresh[None], step_update.reshape(weights.shape), new_weights.reshape(weights.shape)


def solution(mesh):
    fine = Mesh(mesh.devices.reshape(8, 4, 2, 4), ("z", "x", "core", "y"))
    dp = ("z", "x", "core")
    return jax.shard_map(
        on_device,
        mesh=fine,
        in_specs=(
            P(dp, None, "y", None),
            P(dp, None, "y", None),
            P(None, ("y",) + dp, None),
            P(),
        ),
        out_specs=(
            P(dp, None, "y", None),
            P(None, ("y",) + dp, None),
            P(None, ("y",) + dp, None),
        ),
        check_vma=False,
    )
```
